512 devices in a mesh: dp: 32 (over x, y), expert: 8 (over z), tensor: 2 (over core).
Axes of the slice: x: 4, y: 8, z: 8, core: 2. Of those that a mesh axis runs over, the one named last changes fastest.
Arguments:
- tokens: bfloat16 [32768, 2560], P(('dp', 'expert'), 'tensor'), may hold values from -6 to 6
- target: bfloat16 [32768, 2560], P(('dp', 'expert'), 'tensor'), may hold values from -6 to 6
- expert_ids: int32 [32768], P(('dp', 'expert')), may hold values from 0 to 127, as said below
- doc_lengths: int32 [256, 8], P(('dp', 'expert')), may hold values from 1 to 16, as said below
- w_gate: bfloat16 [8, 2560, 8192], P('expert', 'tensor', 'dp'), may hold values from -0.125 to 0.125
- w_up: bfloat16 [8, 2560, 8192], P('expert', 'tensor', 'dp'), may hold values from -0.125 to 0.125
- w_down: bfloat16 [8, 8192, 2560], P('expert', 'dp', 'tensor'), may hold values from -0.0625 to 0.0625
Outputs:
- grad_tokens: bfloat16 [32768, 2560], P(('dp', 'expert'), 'tensor')
- grad_gate: bfloat16 [8, 2560, 8192], P('expert', 'tensor', 'dp')
- grad_up: bfloat16 [8, 2560, 8192], P('expert', 'tensor', 'dp')
- grad_down: bfloat16 [8, 8192, 2560], P('expert', 'dp', 'tensor')
The draws below stay inside these ranges and needn't reach their ends.
Inputs may be any that keep to these rules, and one draw needn't show every extreme that they name: `expert_ids`: among the 128 tokens of one packed row no id appears more than 2 times, and in every row one id below 8 appears exactly 2 times. `doc_lengths`: every row holds a document of 16 tokens; the lengths of a row sum to at most 128.
All inputs are finite; a program needn't handle non-finite values.
Results may differ from the reference program's by a relative error of at most 0.03.
Values may be sent and summed in bfloat16 or wider, within the bound.
No kernel may reach another device: no remote copies, remote signals or barrier semaphores. Data moves between devices by JAX's collectives and lax.ppermute only.
A program may use at most 64 MiB of HBM per device.

```python
import jax
import jax.numpy as jnp
from jax import lax

D = 2560
FF = 8192
EXPERTS = 128
ROW_LEN = 128
DOCS = 8
EXP_WIN = 8
CAP = 2
DOC_MAX = 16
ROWS = 256
TOKENS = 32768
N_DP = 32


def draw_expert_ids(key, part):
    key = jax.random.fold_in(key, 11)

    def one_row(row_key, row_index):
        forced = row_index % EXP_WIN
        first_key, second_key = jax.random.split(row_key)
        others = (jnp.arange((EXPERTS - 1) * CAP, dtype=jnp.int32) // CAP + forced + 1) % EXPERTS
        others = jax.random.permutation(first_key, others)[:ROW_LEN - CAP]
        filled = jnp.concatenate([forced * jnp.ones((CAP,), jnp.int32), others])
        return jax.random.permutation(second_key, filled)
    row_keys = jax.random.split(key, ROWS)
    drawn = jax.vmap(one_row)(row_keys, jnp.arange(ROWS, dtype=jnp.int32))
    return drawn.reshape(TOKENS).astype(jnp.int32)


def draw_doc_lengths(key, part):
    key = jax.random.fold_in(key, 12)
    first_key, second_key = jax.random.split(key)
    lengths = jax.random.randint(first_key, (ROWS, DOCS), 1, DOC_MAX + 1)
    column = jax.random.randint(second_key, (ROWS, 1), 0, DOCS)
    chosen = jnp.arange(DOCS, dtype=jnp.int32)[None, :] == column
    return jnp.where(chosen, DOC_MAX, lengths).astype(jnp.int32)


def level_of(key, dims, cuts, low, top_value):
    gain = 1.0
    for dim, shards_of in cuts:
        heights = jax.random.uniform(jax.random.fold_in(jax.random.fold_in(key, 6), dim), (shards_of,), jnp.float32, low / len(cuts), top_value / len(cuts))
        gain = gain * jnp.repeat(jnp.exp(heights), dims[dim] // shards_of).reshape((-1,) + (1,) * (len(dims) - 1 - dim))
    return gain


def noise(rng, shape, scale, bound, cuts=(), held_as=jnp.bfloat16):
    values = scale * jax.random.normal(rng, shape, jnp.float32)
    if cuts:
        values = values * level_of(rng, shape, cuts, -0.22, 0.18)
    return jnp.clip(values, -bound, bound).astype(held_as)


def setup_inputs(seed: int = 0) -> dict:
    keys = jax.random.split(jax.random.key(seed), 8)
    return {
        "tokens": noise(keys[0], (TOKENS, D), 1.0, 6.0, ((0, 256), (1, 2))),
        "target": noise(keys[1], (TOKENS, D), 1.0, 6.0, ((0, 256), (1, 2))),
        "expert_ids": draw_expert_ids(jax.random.fold_in(keys[7], 71), 0),
        "doc_lengths": draw_doc_lengths(jax.random.fold_in(keys[7], 71), 0),
        "w_gate": noise(keys[4], (EXP_WIN, D, FF), D ** -0.5, 0.125, ((0, 8), (1, 2), (2, 32))),
        "w_up": noise(keys[5], (EXP_WIN, D, FF), D ** -0.5, 0.125, ((0, 8), (1, 2), (2, 32))),
        "w_down": noise(keys[6], (EXP_WIN, FF, D), FF ** -0.5, 0.0625, ((0, 8), (1, 32), (2, 2))),
    }


def silu_slope(gate_val):
    sig = jax.nn.sigmoid(gate_val)
    return sig * (1.0 + gate_val * (1.0 - sig))


def dispatch_rows(placed, values):
    moved = jnp.einsum('brec,brd->ebcd', placed, values.astype(jnp.float32))
    return moved.astype(jnp.bfloat16).reshape(EXP_WIN, ROWS * CAP, D)


def combine_rows(placed, expert_rows):
    slots = expert_rows.reshape(EXP_WIN, ROWS, CAP, D).astype(jnp.float32)
    return jnp.einsum('brec,ebcd->brd', placed, slots)


def expert_hidden(row_data, gate_w, up_w):
    gate_val = jnp.dot(row_data, gate_w, preferred_element_type=jnp.float32)
    up_val = jnp.dot(row_data, up_w, preferred_element_type=jnp.float32)
    hidden = (jax.nn.silu(gate_val) * up_val).astype(jnp.bfloat16)
    return gate_val, up_val, hidden


def down_blocks(hidden, down_w):
    block = FF // N_DP
    left = hidden.reshape(ROWS * CAP, N_DP, block).astype(jnp.float32)
    right = down_w.reshape(N_DP, block, D).astype(jnp.float32)
    parts = jnp.einsum('rkf,kfd->krd', left, right).astype(jnp.bfloat16)
    return jnp.sum(parts.astype(jnp.float32), axis=0).astype(jnp.bfloat16)


def input_blocks(gate_grad, up_grad, gate_w, up_w):
    block = FF // N_DP
    gate_left = gate_grad.reshape(ROWS * CAP, N_DP, block).astype(jnp.float32)
    up_left = up_grad.reshape(ROWS * CAP, N_DP, block).astype(jnp.float32)
    gate_right = gate_w.reshape(D, N_DP, block).astype(jnp.float32)
    up_right = up_w.reshape(D, N_DP, block).astype(jnp.float32)
    parts = jnp.einsum('rkf,dkf->krd', gate_left, gate_right) + jnp.einsum('rkf,dkf->krd', up_left, up_right)
    parts = parts.astype(jnp.bfloat16)
    return jnp.sum(parts.astype(jnp.float32), axis=0).astype(jnp.bfloat16)


def reference(tokens, target, expert_ids, doc_lengths, w_gate, w_up, w_down):
    values = tokens.reshape(ROWS, ROW_LEN, D)
    teacher = target.reshape(ROWS, ROW_LEN, D)
    ids = expert_ids.reshape(ROWS, ROW_LEN)
    live_mask = (jnp.arange(ROW_LEN)[None, :] < jnp.sum(doc_lengths, axis=1)[:, None]).astype(jnp.float32)
    one_hot = (ids[:, :, None] == jnp.arange(EXP_WIN)[None, None, :]).astype(jnp.int32)
    order_rank = jnp.cumsum(one_hot, axis=1) - 1
    placed = ((one_hot[..., None] == 1) & (order_rank[..., None] == jnp.arange(CAP)[None, None, None, :])).astype(jnp.float32)
    row_data = dispatch_rows(placed, values)

    def forward_one(items):
        rows_e, gate_w, up_w, down_w = items
        gate_val, up_val, hidden = expert_hidden(rows_e, gate_w, up_w)
        return down_blocks(hidden, down_w)

    expert_rows = lax.map(forward_one, (row_data, w_gate, w_up, w_down))
    output = values.astype(jnp.float32) + combine_rows(placed, expert_rows)
    residual_grad = (live_mask[..., None] * (output - teacher.astype(jnp.float32))).astype(jnp.bfloat16)
    grad_rows = dispatch_rows(placed, residual_grad)

    def backward_one(items):
        rows_e, grads_e, gate_w, up_w, down_w = items
        gate_val, up_val, hidden = expert_hidden(rows_e, gate_w, up_w)
        hidden_grad = jnp.dot(grads_e, down_w.T, preferred_element_type=jnp.float32)
        gate_grad = (hidden_grad * up_val * silu_slope(gate_val)).astype(jnp.bfloat16)
        up_grad = (hidden_grad * jax.nn.silu(gate_val)).astype(jnp.bfloat16)
        down_out = jnp.dot(hidden.T, grads_e, preferred_element_type=jnp.float32).astype(jnp.bfloat16)
        gate_out = jnp.dot(rows_e.T, gate_grad, preferred_element_type=jnp.float32).astype(jnp.bfloat16)
        up_out = jnp.dot(rows_e.T, up_grad, preferred_element_type=jnp.float32).astype(jnp.bfloat16)
        input_rows = input_blocks(gate_grad, up_grad, gate_w, up_w)
        return input_rows, gate_out, up_out, down_out

    input_rows, grad_gate, grad_up, grad_down = lax.map(backward_one, (row_data, grad_rows, w_gate, w_up, w_down))
    grad_tokens = residual_grad.astype(jnp.float32) + combine_rows(placed, input_rows)
    grad_tokens = grad_tokens.astype(jnp.bfloat16).reshape(TOKENS, D)
    return (grad_tokens, grad_gate, grad_up, grad_down)
```

```python
import jax
import jax.numpy as jnp
from jax import lax
from jax.sharding import Mesh, PartitionSpec as P

CAP = 2
NX, NY, NZ = 4, 8, 8
F32, BF16 = jnp.float32, jnp.bfloat16
CONTRACT_ROWS = (((0,), (0,)), ((), ()))
CONTRACT_COLS = (((1,), (1,)), ((), ()))


def silu_slope(gate_val):
    sig = jax.nn.sigmoid(gate_val)
    return sig * (1.0 + gate_val * (1.0 - sig))


def ring(value, axis, size, shift):
    return lax.ppermute(value, axis, [(i, (i + shift) % size) for i in range(size)])


def swap_add(part):
    mine = part.astype(BF16)
    other = lax.ppermute(mine, "c", [(0, 1), (1, 0)])
    return mine.astype(F32) + other.astype(F32)


def spread(rows):
    blocks = jnp.broadcast_to(rows[None], (NY,) + rows.shape)
    column = lax.all_to_all(blocks, "y", 0, 0, tiled=True).reshape(NY * rows.shape[0], rows.shape[1])
    return [column] + [ring(column, "x", NX, s) for s in SHIFTS]


SHIFTS = (1, 3, 2)


def gather_x(parts):
    total = parts[0].astype(F32)
    for s, part in zip(SHIFTS, parts[1:]):
        total = total + ring(part.astype(BF16), "x", NX, NX - s).astype(F32)
    return total


def local(tokens, target, expert_ids, doc_lengths, w_gate, w_up, w_down):
    row_len, features = tokens.shape
    slot_count = NZ * CAP
    w_gate, w_up, w_down = w_gate[0], w_up[0], w_down[0]
    live = jnp.arange(row_len) < jnp.sum(doc_lengths)
    one_hot = (expert_ids[:, None] == jnp.arange(NZ)[None, :]).astype(jnp.int32)
    order_rank = jnp.cumsum(one_hot, axis=0) - 1
    placed = (one_hot[:, :, None] == 1) & (order_rank[:, :, None] == jnp.arange(CAP)[None, None, :])
    placed = placed & live[:, None, None]
    select = placed.reshape(row_len, slot_count).astype(BF16)

    def to_slots(values):
        moved = lax.dot_general(select, values, CONTRACT_ROWS, preferred_element_type=F32)
        return moved.astype(BF16).reshape(NZ, CAP, features)

    both = jnp.concatenate([to_slots(tokens), to_slots(target)], axis=1)
    arrived = lax.all_to_all(both, "z", 0, 0, tiled=True)
    my_rows = arrived[:, :CAP].reshape(slot_count, features)
    my_target = arrived[:, CAP:].reshape(slot_count, features)

    chunks = spread(my_rows)
    gates, ups, hiddens, parts = [], [], [], []
    for rows in chunks:
        gate_part = jnp.dot(rows, w_gate, preferred_element_type=F32)
        up_part = jnp.dot(rows, w_up, preferred_element_type=F32)
        summed = swap_add(jnp.concatenate([gate_part, up_part], axis=1))
        gate_val, up_val = summed[:, : w_gate.shape[1]], summed[:, w_gate.shape[1] :]
        hidden = (jax.nn.silu(gate_val) * up_val).astype(BF16)
        gates.append(gate_val)
        ups.append(up_val)
        hiddens.append(hidden)
        parts.append(jnp.dot(hidden, w_down, preferred_element_type=F32).astype(BF16))
    column = gather_x(parts).astype(BF16).reshape(NY, slot_count, features)
    pieces = lax.all_to_all(column, "y", 0, 0, tiled=True)
    expert_rows = jnp.sum(pieces.astype(F32), axis=0).astype(BF16)
    residual = (my_rows.astype(F32) + expert_rows.astype(F32) - my_target.astype(F32)).astype(BF16)

    grad_chunks = spread(residual)
    gate_grads, up_grads, parts = [], [], []
    for i, grads in enumerate(grad_chunks):
        hidden_grad = swap_add(lax.dot_general(grads, w_down, CONTRACT_COLS, preferred_element_type=F32))
        gate_grad = (hidden_grad * ups[i] * silu_slope(gates[i])).astype(BF16)
        up_grad = (hidden_grad * jax.nn.silu(gates[i])).astype(BF16)
        gate_grads.append(gate_grad)
        up_grads.append(up_grad)
        first = lax.dot_general(gate_grad, w_gate, CONTRACT_COLS, preferred_element_type=F32)
        second = lax.dot_general(up_grad, w_up, CONTRACT_COLS, preferred_element_type=F32)
        parts.append((first + second).astype(BF16))
    mine = (jnp.arange(NY * slot_count) // slot_count) == lax.axis_index("y")
    column = gather_x(parts) + jnp.where(mine[:, None], grad_chunks[0].astype(F32), 0.0)
    pieces = lax.all_to_all(
        column.astype(BF16).reshape(NY * NZ, CAP, features), ("y", "z"), 0, 0, tiled=True
    )
    slots = jnp.sum(pieces.reshape(NY, slot_count, features).astype(F32), axis=0).astype(BF16)

    all_rows = jnp.concatenate(chunks, axis=0)
    all_grads = jnp.concatenate(grad_chunks, axis=0)

    def weight_grad(left, right):
        return lax.dot_general(left, right, CONTRACT_ROWS, preferred_element_type=F32).astype(BF16)

    grad_down = weight_grad(jnp.concatenate(hiddens, axis=0), all_grads)
    grad_gate = weight_grad(all_rows, jnp.concatenate(gate_grads, axis=0))
    grad_up = weight_grad(all_rows, jnp.concatenate(up_grads, axis=0))

    routed = jnp.dot(select, slots, preferred_element_type=F32)
    unrouted = live & ~jnp.any(placed, axis=(1, 2))
    own = jnp.where(unrouted[:, None], tokens.astype(F32) - target.astype(F32), 0.0)
    grad_tokens = (own + routed).astype(BF16)
    return (grad_tokens, grad_gate[None], grad_up[None], grad_down[None])


def solution(mesh):
    cube = Mesh(mesh.devices.reshape(NX, NY, NZ, 2), ("x", "y", "z", "c"))
    token_spec = P(("x", "y", "z"), "c")
    in_spec, out_spec = P("z", "c", ("x", "y")), P("z", ("x", "y"), "c")
    return jax.shard_map(
        local,
        mesh=cube,
        in_specs=(token_spec, token_spec, P(("x", "y", "z")), P(("x", "y", "z"), None), in_spec, in_spec, out_spec),
        out_specs=(token_spec, in_spec, in_spec, out_spec),
        check_vma=False,
    )
```

```python
import jax
import jax.numpy as jnp
from jax import lax
from jax.experimental import pallas as pl
from jax.experimental.pallas import tpu as pltpu
from jax.sharding import Mesh, PartitionSpec as P

CAP = 2
NX, NY, NZ = 4, 8, 8
F32, BF16 = jnp.float32, jnp.bfloat16
CONTRACT_ROWS = (((0,), (0,)), ((), ()))
CONTRACT_COLS = (((1,), (1,)), ((), ()))
SWAP = [(0, 1), (1, 0)]
PAIR = [(0, 1), (1, 0), (2, 3), (3, 2)]
CROSS = [(0, 3), (3, 0), (1, 2), (2, 1)]


def silu_slope(gate_val):
    sig = jax.nn.sigmoid(gate_val)
    return sig * (1.0 + gate_val * (1.0 - sig))


def iota(shape, dim):
    return lax.broadcasted_iota(jnp.int32, shape, dim)


def one_hot(mask):
    return jnp.where(mask, 1.0, 0.0).astype(BF16)


def slot_matrix(ids, lengths, count, per_expert):
    tokens = ids.shape[1]
    slot = iota((count, tokens), 0)
    mine = ids == slot // per_expert
    before = iota((tokens, tokens), 0) < iota((tokens, tokens), 1)
    rank = jnp.dot(one_hot(mine), one_hot(before), preferred_element_type=F32)
    live = iota((count, tokens), 1) < jnp.sum(lengths, axis=1, keepdims=True)
    return mine & live & (rank == (slot % CAP).astype(F32))


def dispatch_kernel(ids_ref, lengths_ref, tokens_ref, target_ref, out_ref):
    experts, lines, half = out_ref.shape
    chosen = slot_matrix(ids_ref[...], lengths_ref[...], experts * lines, lines)
    line = iota(chosen.shape, 0) % lines
    from_target = line % (2 * CAP) >= CAP
    pick_tokens, pick_target = one_hot(chosen & ~from_target), one_hot(chosen & from_target)

    def moved(cols):
        out = jnp.dot(pick_tokens, tokens_ref[:, cols], preferred_element_type=F32)
        return out + jnp.dot(pick_target, target_ref[:, cols], preferred_element_type=F32)

    first = iota((experts * lines, half), 0) % lines < 2 * CAP
    both = jnp.where(first, moved(slice(0, half)), moved(slice(half, 2 * half)))
    out_ref[...] = both.reshape(experts, lines, half).astype(BF16)


def arrive_kernel(arrived_ref, blocks_ref, rows_ref, target_ref):
    experts, lines, half = arrived_ref.shape
    count = rows_ref.shape[0]
    arrived = arrived_ref[...].astype(F32).reshape(experts * lines, half).astype(BF16)
    row, line = iota((count, experts * lines), 0), iota((count, experts * lines), 1)

    def rows(offset):
        parts = []
        for start in (offset, offset + 2 * CAP):
            pick = one_hot(line == row // CAP * lines + row % CAP + start)
            parts.append(jnp.dot(pick, arrived, preferred_element_type=F32).astype(BF16))
        return jnp.concatenate(parts, axis=1)

    mine = rows(0)
    rows_ref[...] = mine
    target_ref[...] = rows(CAP)
    blocks_ref[...] = jnp.broadcast_to(mine[None], blocks_ref.shape)


def settle_kernel(pieces_ref, rows_ref, target_ref, blocks_ref):
    total = pieces_ref[0].astype(F32)
    for i in range(1, pieces_ref.shape[0]):
        total += pieces_ref[i].astype(F32)
    output = rows_ref[...].astype(F32) + total.astype(BF16).astype(F32)
    residual = (output - target_ref[...].astype(F32)).astype(BF16)
    blocks_ref[...] = jnp.broadcast_to(residual[None], blocks_ref.shape)


def combine_kernel(ids_ref, lengths_ref, tokens_ref, target_ref, pieces_ref, out_ref):
    row_len = tokens_ref.shape[0]
    count = pieces_ref.shape[1]
    chosen = one_hot(slot_matrix(ids_ref[...], lengths_ref[...], count, CAP))
    slots = pieces_ref[0].astype(F32)
    for i in range(1, pieces_ref.shape[0]):
        slots += pieces_ref[i].astype(F32)
    routed = lax.dot_general(chosen, slots.astype(BF16), CONTRACT_ROWS, preferred_element_type=F32)
    taken = lax.dot_general(chosen, jnp.ones((count, 128), BF16), CONTRACT_ROWS, preferred_element_type=F32)[:, :1]
    live = iota((row_len, 1), 0) < jnp.sum(lengths_ref[...], axis=1, keepdims=True)
    own = tokens_ref[...].astype(F32) - target_ref[...].astype(F32)
    out_ref[...] = (jnp.where(live & (taken == 0.0), own, 0.0) + routed).astype(BF16)


def array(*shape, dtype=BF16):
    return jax.ShapeDtypeStruct(shape, dtype)


def swap(value):
    return lax.ppermute(value, "c", SWAP)


def pair(value):
    return lax.ppermute(value, "x", PAIR)


def cross(value):
    return lax.ppermute(value, "x", CROSS)


def after(value, early):
    return lax.optimization_barrier((value, early))


def over_y(blocks):
    return lax.all_to_all(blocks, "y", 0, 0, tiled=True)


def times(left, right):
    return jnp.dot(left, right, preferred_element_type=F32)


def times_t(left, right):
    return lax.dot_general(left, right, CONTRACT_COLS, preferred_element_type=F32)


def stack(*parts):
    return jnp.concatenate(parts, axis=0)


def beside(*parts):
    return jnp.concatenate(parts, axis=1)


def weight_grad(left, right):
    return lax.dot_general(left, right, CONTRACT_ROWS, preferred_element_type=F32).astype(BF16)


def local(tokens, target, expert_ids, doc_lengths, w_gate, w_up, w_down):
    row_len, features = tokens.shape
    slot_count = NZ * CAP
    column_rows = NY * slot_count
    gate_w, up_w, down_w = w_gate[0], w_up[0], w_down[0]
    units = gate_w.shape[1]
    ids = expert_ids.reshape(1, row_len)

    message = pl.pallas_call(dispatch_kernel, out_shape=array(NZ, 4 * CAP, features // 2))(
        ids, doc_lengths, tokens, target
    )
    arrived = lax.all_to_all(message, "z", 0, 0, tiled=True)
    blocks, my_rows, my_target = pl.pallas_call(
        arrive_kernel,
        out_shape=(array(NY, slot_count, features), array(slot_count, features), array(slot_count, features)),
    )(arrived)

    blocks, gate_w_p = after(blocks, pair(gate_w))
    column = over_y(blocks).reshape(column_rows, features)
    column, up_w_p = after(column, pair(up_w))

    def products(rows):
        return beside(*[times(rows, w).astype(BF16) for w in (gate_w, up_w, gate_w_p, up_w_p)])

    crossed = cross(column)
    part = stack(products(column), products(crossed))
    part, down_w_p = after(part, pair(down_w))
    sums = part.astype(F32) + swap(part).astype(F32)
    gate, up, gate_p, up_p = jnp.split(sums, 4, axis=1)
    hidden = (jax.nn.silu(gate) * up).astype(BF16)
    hidden_p = (jax.nn.silu(gate_p) * up_p).astype(BF16)

    def column_sum(product):
        theirs = cross(product(slice(column_rows, None)).astype(BF16))
        return product(slice(0, column_rows)) + theirs.astype(F32)

    column_out = column_sum(lambda s: times(hidden[s], down_w) + times(hidden_p[s], down_w_p)).astype(BF16)
    column_out, pair_column = after(column_out, pair(column))
    pieces = over_y(column_out.reshape(NY, slot_count, features))
    blocks = pl.pallas_call(settle_kernel, out_shape=array(NY, slot_count, features))(pieces, my_rows, my_target)
    blocks, pair_crossed = after(blocks, pair(crossed))

    grad_column = over_y(blocks).reshape(column_rows, features)
    grad_column, pair_hidden = after(grad_column, pair(hidden_p))
    grad_crossed = cross(grad_column)
    part = stack(
        *[beside(*[times_t(g, w).astype(BF16) for w in (down_w, down_w_p)]) for g in (grad_column, grad_crossed)]
    )
    part, pair_grad_column = after(part, pair(grad_column))
    sums = part.astype(F32) + swap(part).astype(F32)
    back, back_p = jnp.split(sums, 2, axis=1)
    gate_grad = (back * up * silu_slope(gate)).astype(BF16)
    up_grad = (back * jax.nn.silu(gate)).astype(BF16)
    gate_grad_p = (back_p * up_p * silu_slope(gate_p)).astype(BF16)
    up_grad_p = (back_p * jax.nn.silu(gate_p)).astype(BF16)

    def input_part(s):
        own = times_t(gate_grad[s], gate_w) + times_t(up_grad[s], up_w)
        return own + times_t(gate_grad_p[s], gate_w_p) + times_t(up_grad_p[s], up_w_p)

    mine = (jnp.arange(column_rows) // slot_count) == lax.axis_index("y")
    column_in = column_sum(input_part) + jnp.where(mine[:, None], grad_column.astype(F32), 0.0)
    column_in, pair_grad_crossed = after(column_in.astype(BF16), pair(grad_crossed))
    pair_in = pair(beside(gate_grad_p, up_grad_p))
    pieces = lax.all_to_all(column_in.reshape(NY * NZ, CAP, features), ("y", "z"), 0, 0, tiled=True)
    grad_tokens = pl.pallas_call(combine_kernel, out_shape=array(row_len, features))(
        ids, doc_lengths, tokens, target, pieces.reshape(NY, slot_count, features)
    )

    rows = stack(column, crossed, pair_column, pair_crossed)
    grads = stack(grad_column, grad_crossed, pair_grad_column, pair_grad_crossed)
    grad_down = weight_grad(stack(hidden, pair_hidden), grads)
    grad_gate = weight_grad(rows, stack(gate_grad, pair_in[:, :units]))
    grad_up = weight_grad(rows, stack(up_grad, pair_in[:, units:]))
    return (grad_tokens, grad_gate[None], grad_up[None], grad_down[None])


def solution(mesh):
    cube = Mesh(mesh.devices.reshape(NX, NY, NZ, 2), ("x", "y", "z", "c"))
    token_spec = P(("x", "y", "z"), "c")
    in_spec, out_spec = P("z", "c", ("x", "y")), P("z", ("x", "y"), "c")
    return jax.shard_map(
        local,
        mesh=cube,
        in_specs=(token_spec, token_spec, P(("x", "y", "z")), P(("x", "y", "z"), None), in_spec, in_spec, out_spec),
        out_specs=(token_spec, in_spec, in_spec, out_spec),
        check_vma=False,
    )
```

```python
import jax
import jax.numpy as jnp
from jax import lax
from jax.experimental import pallas as pl
from jax.experimental.pallas import tpu as pltpu
from jax.sharding import Mesh, PartitionSpec as P

CAP = 2
NX, NY, NZ = 4, 8, 8
F32, BF16 = jnp.float32, jnp.bfloat16
CONTRACT_ROWS = (((0,), (0,)), ((), ()))
CONTRACT_COLS = (((1,), (1,)), ((), ()))
SWAP = [(0, 1), (1, 0)]
PAIR = [(0, 1), (1, 0), (2, 3), (3, 2)]
CROSS = [(0, 3), (3, 0), (1, 2), (2, 1)]
TWO_COLUMNS = [[x * NY + y for x in columns for y in range(NY)] for columns in ((0, 3), (1, 2))]


def silu_slope(gate_val):
    sig = jax.nn.sigmoid(gate_val)
    return sig * (1.0 + gate_val * (1.0 - sig))


def iota(shape, dim):
    return lax.broadcasted_iota(jnp.int32, shape, dim)


def one_hot(mask):
    return jnp.where(mask, 1.0, 0.0).astype(BF16)


def slot_matrix(ids, lengths, count, per_expert):
    tokens = ids.shape[1]
    slot = iota((count, tokens), 0)
    mine = ids == slot // per_expert
    before = iota((tokens, tokens), 0) < iota((tokens, tokens), 1)
    rank = jnp.dot(one_hot(mine), one_hot(before), preferred_element_type=F32)
    live = iota((count, tokens), 1) < jnp.sum(lengths, axis=1, keepdims=True)
    return mine & live & (rank == (slot % CAP).astype(F32))


def dispatch_kernel(ids_ref, lengths_ref, tokens_ref, target_ref, out_ref):
    experts, lines, half = out_ref.shape
    chosen = slot_matrix(ids_ref[...], lengths_ref[...], experts * lines, lines)
    line = iota(chosen.shape, 0) % lines
    from_target = line % (2 * CAP) >= CAP
    pick_tokens, pick_target = one_hot(chosen & ~from_target), one_hot(chosen & from_target)

    def moved(cols):
        out = jnp.dot(pick_tokens, tokens_ref[:, cols], preferred_element_type=F32)
        return out + jnp.dot(pick_target, target_ref[:, cols], preferred_element_type=F32)

    first = iota((experts * lines, half), 0) % lines < 2 * CAP
    both = jnp.where(first, moved(slice(0, half)), moved(slice(half, 2 * half)))
    out_ref[...] = both.reshape(experts, lines, half).astype(BF16)


def arrive_kernel(arrived_ref, blocks_ref, rows_ref, target_ref):
    experts, lines, half = arrived_ref.shape
    count = rows_ref.shape[0]
    arrived = arrived_ref[...].astype(F32).reshape(experts * lines, half).astype(BF16)
    row, line = iota((count, experts * lines), 0), iota((count, experts * lines), 1)

    def rows(offset):
        parts = []
        for start in (offset, offset + 2 * CAP):
            pick = one_hot(line == row // CAP * lines + row % CAP + start)
            parts.append(jnp.dot(pick, arrived, preferred_element_type=F32).astype(BF16))
        return jnp.concatenate(parts, axis=1)

    mine = rows(0)
    rows_ref[...] = mine
    target_ref[...] = rows(CAP)
    blocks_ref[...] = jnp.broadcast_to(mine[None], blocks_ref.shape)


def settle_kernel(pieces_ref, rows_ref, target_ref, blocks_ref):
    total = pieces_ref[0].astype(F32)
    for i in range(1, pieces_ref.shape[0]):
        total += pieces_ref[i].astype(F32)
    output = rows_ref[...].astype(F32) + total.astype(BF16).astype(F32)
    residual = (output - target_ref[...].astype(F32)).astype(BF16)
    blocks_ref[...] = jnp.broadcast_to(residual[None], blocks_ref.shape)


def own_kernel(ids_ref, lengths_ref, tokens_ref, target_ref, own_ref, chosen_ref):
    row_len = tokens_ref.shape[0]
    chosen = one_hot(slot_matrix(ids_ref[...], lengths_ref[...], chosen_ref.shape[0], CAP))
    taken = times_rows(chosen, jnp.ones((chosen.shape[0], 128), BF16))[:, :1]
    live = iota((row_len, 1), 0) < jnp.sum(lengths_ref[...], axis=1, keepdims=True)
    own = tokens_ref[...].astype(F32) - target_ref[...].astype(F32)
    own_ref[...] = jnp.where(live & (taken == 0.0), own, 0.0).astype(BF16)
    chosen_ref[...] = chosen


def combine_kernel(own_ref, chosen_ref, pieces_ref, out_ref):
    slots = pieces_ref[0].astype(F32)
    for i in range(1, pieces_ref.shape[0]):
        slots += pieces_ref[i].astype(F32)
    routed = times_rows(chosen_ref[...], slots.astype(BF16))
    out_ref[...] = (own_ref[...].astype(F32) + routed).astype(BF16)


def times_rows(left, right):
    return lax.dot_general(left, right, CONTRACT_ROWS, preferred_element_type=F32)


def array(*shape, dtype=BF16):
    return jax.ShapeDtypeStruct(shape, dtype)


def swap(value):
    return lax.ppermute(value, "c", SWAP)


def pair(value):
    return lax.ppermute(value, "x", PAIR)


def cross(value):
    return lax.ppermute(value, "x", CROSS)


def after(*values):
    return lax.optimization_barrier(values)


def over_y(blocks):
    return lax.all_to_all(blocks, "y", 0, 0, tiled=True)


def over_two_columns(blocks):
    return lax.all_to_all(blocks, ("x", "y"), 0, 0, axis_index_groups=TWO_COLUMNS, tiled=True)


def in_order(mine, theirs):
    lower = lax.axis_index("x") < NX // 2
    return jnp.where(lower, mine, theirs), jnp.where(lower, theirs, mine)


def times(left, right):
    return jnp.dot(left, right, preferred_element_type=F32)


def times_t(left, right):
    return lax.dot_general(left, right, CONTRACT_COLS, preferred_element_type=F32)


def stack(*parts):
    return jnp.concatenate(parts, axis=0)


def beside(*parts):
    return jnp.concatenate(parts, axis=1)


def weight_grad(left, right):
    return times_rows(left, right).astype(BF16)


def local(tokens, target, expert_ids, doc_lengths, w_gate, w_up, w_down):
    row_len, features = tokens.shape
    slot_count = NZ * CAP
    column_rows = NY * slot_count
    gate_w, up_w, down_w = w_gate[0], w_up[0], w_down[0]
    units = gate_w.shape[1]
    ids = expert_ids.reshape(1, row_len)

    message = pl.pallas_call(dispatch_kernel, out_shape=array(NZ, 4 * CAP, features // 2))(
        ids, doc_lengths, tokens, target
    )
    arrived = lax.all_to_all(message, "z", 0, 0, tiled=True)
    blocks, my_rows, my_target = pl.pallas_call(
        arrive_kernel,
        out_shape=(array(NY, slot_count, features), array(slot_count, features), array(slot_count, features)),
    )(arrived)

    blocks, gate_w_p = after(blocks, pair(gate_w))
    column = over_y(blocks).reshape(column_rows, features)
    column, up_w_p = after(column, pair(up_w))

    def products(rows):
        return beside(*[times(rows, w).astype(BF16) for w in (gate_w, up_w, gate_w_p, up_w_p)])

    crossed = cross(column)
    part = stack(products(column), products(crossed))
    part, down_w_p = after(part, pair(down_w))
    sums = part.astype(F32) + swap(part).astype(F32)
    gate, up, gate_p, up_p = jnp.split(sums, 4, axis=1)
    hidden = (jax.nn.silu(gate) * up).astype(BF16)
    hidden_p = (jax.nn.silu(gate_p) * up_p).astype(BF16)

    mine, theirs = slice(0, column_rows), slice(column_rows, None)

    def output_part(s):
        return times(hidden[s], down_w) + times(hidden_p[s], down_w_p)

    partial = stack(*in_order(output_part(mine).astype(BF16), output_part(theirs).astype(BF16)))
    partial, tokens_late, target_late = after(partial, tokens, target)
    own, chosen = pl.pallas_call(own_kernel, out_shape=(array(row_len, features), array(slot_count, row_len)))(
        ids, doc_lengths, tokens_late, target_late
    )
    pieces = over_two_columns(partial.reshape(2 * NY, slot_count, features))
    pieces, own, chosen = after(pieces, own, chosen)
    blocks = pl.pallas_call(settle_kernel, out_shape=array(2 * NY, slot_count, features))(pieces, my_rows, my_target)
    blocks, pair_column = after(blocks, pair(column))

    both = over_two_columns(blocks).reshape(2 * column_rows, features)
    both, pair_crossed = after(both, pair(crossed))
    grad_column, grad_crossed = in_order(both[:column_rows], both[column_rows:])
    part = stack(
        *[beside(*[times_t(g, w).astype(BF16) for w in (down_w, down_w_p)]) for g in (grad_column, grad_crossed)]
    )
    down_part, down_part_p = [
        times_rows(h[:column_rows], grad_column) + times_rows(h[column_rows:], grad_crossed) for h in (hidden, hidden_p)
    ]
    sums = part.astype(F32) + swap(part).astype(F32)
    back, back_p = jnp.split(sums, 2, axis=1)
    gate_grad = (back * up * silu_slope(gate)).astype(BF16)
    up_grad = (back * jax.nn.silu(gate)).astype(BF16)
    gate_grad_p = (back_p * up_p * silu_slope(gate_p)).astype(BF16)
    up_grad_p = (back_p * jax.nn.silu(gate_p)).astype(BF16)

    def input_part(s):
        own = times_t(gate_grad[s], gate_w) + times_t(up_grad[s], up_w)
        return own + times_t(gate_grad_p[s], gate_w_p) + times_t(up_grad_p[s], up_w_p)

    at_home = (jnp.arange(column_rows) // slot_count) == lax.axis_index("y")
    extra = jnp.where(at_home[:, None], grad_column.astype(F32), 0.0)
    partial = input_part(theirs).astype(BF16)
    partial, down_part_late = after(partial, down_part_p.astype(BF16))
    column_in = input_part(mine) + extra + cross(partial).astype(F32)
    pair_down = pair(down_part_late)
    column_in, pair_in = after(column_in.astype(BF16), pair(beside(gate_grad_p, up_grad_p)))
    pieces = lax.all_to_all(column_in.reshape(NY * NZ, CAP, features), ("y", "z"), 0, 0, tiled=True)
    grad_tokens = pl.pallas_call(combine_kernel, out_shape=array(row_len, features))(
        own, chosen, pieces.reshape(NY, slot_count, features)
    )

    rows = stack(column, crossed, pair_column, pair_crossed)
    grad_down = (down_part + pair_down.astype(F32)).astype(BF16)
    grad_gate = weight_grad(rows, stack(gate_grad, pair_in[:, :units]))
    grad_up = weight_grad(rows, stack(up_grad, pair_in[:, units:]))
    return (grad_tokens, grad_gate[None], grad_up[None], grad_down[None])


def solution(mesh):
    cube = Mesh(mesh.devices.reshape(NX, NY, NZ, 2), ("x", "y", "z", "c"))
    token_spec = P(("x", "y", "z"), "c")
    in_spec, out_spec = P("z", "c", ("x", "y")), P("z", ("x", "y"), "c")
    return jax.shard_map(
        local,
        mesh=cube,
        in_specs=(token_spec, token_spec, P(("x", "y", "z")), P(("x", "y", "z"), None), in_spec, in_spec, out_spec),
        out_specs=(token_spec, in_spec, in_spec, out_spec),
        check_vma=False,
    )
```

```python
import jax
import jax.numpy as jnp
from jax import lax
from jax.experimental import pallas as pl
from jax.experimental.pallas import tpu as pltpu
from jax.sharding import Mesh, PartitionSpec as P

CAP = 2
NX, NY, NZ = 4, 8, 8
F32, BF16 = jnp.float32, jnp.bfloat16
CONTRACT_ROWS = (((0,), (0,)), ((), ()))
CONTRACT_COLS = (((1,), (1,)), ((), ()))
SWAP = [(0, 1), (1, 0)]
PAIR = [(0, 1), (1, 0), (2, 3), (3, 2)]
CROSS = [(0, 3), (3, 0), (1, 2), (2, 1)]
TWO_COLUMNS = [[x * NY + y for x in columns for y in range(NY)] for columns in ((0, 3), (1, 2))]


def silu_slope(gate_val):
    sig = jax.nn.sigmoid(gate_val)
    return sig * (1.0 + gate_val * (1.0 - sig))


def iota(shape, dim):
    return lax.broadcasted_iota(jnp.int32, shape, dim)


def one_hot(mask):
    return jnp.where(mask, 1.0, 0.0).astype(BF16)


def slot_matrix(ids, lengths, count, per_expert):
    tokens = ids.shape[1]
    slot = iota((count, tokens), 0)
    mine = ids == slot // per_expert
    before = iota((tokens, tokens), 0) < iota((tokens, tokens), 1)
    rank = jnp.dot(one_hot(mine), one_hot(before), preferred_element_type=F32)
    live = iota((count, tokens), 1) < jnp.sum(lengths, axis=1, keepdims=True)
    return mine & live & (rank == (slot % CAP).astype(F32))


def dispatch_kernel(ids_ref, lengths_ref, tokens_ref, target_ref, out_ref):
    experts, lines, half = out_ref.shape
    chosen = slot_matrix(ids_ref[...], lengths_ref[...], experts * lines, lines)
    line = iota(chosen.shape, 0) % lines
    from_target = line % (2 * CAP) >= CAP
    pick_tokens, pick_target = one_hot(chosen & ~from_target), one_hot(chosen & from_target)

    def moved(cols):
        out = jnp.dot(pick_tokens, tokens_ref[:, cols], preferred_element_type=F32)
        return out + jnp.dot(pick_target, target_ref[:, cols], preferred_element_type=F32)

    first = iota((experts * lines, half), 0) % lines < 2 * CAP
    both = jnp.where(first, moved(slice(0, half)), moved(slice(half, 2 * half)))
    out_ref[...] = both.reshape(experts, lines, half).astype(BF16)


def arrive_kernel(arrived_ref, blocks_ref, rows_ref, target_ref):
    experts, lines, half = arrived_ref.shape
    count = rows_ref.shape[0]
    arrived = arrived_ref[...].astype(F32).reshape(experts * lines, half).astype(BF16)
    row, line = iota((count, experts * lines), 0), iota((count, experts * lines), 1)

    def rows(offset):
        parts = []
        for start in (offset, offset + 2 * CAP):
            pick = one_hot(line == row // CAP * lines + row % CAP + start)
            parts.append(jnp.dot(pick, arrived, preferred_element_type=F32).astype(BF16))
        return jnp.concatenate(parts, axis=1)

    mine = rows(0)
    rows_ref[...] = mine
    target_ref[...] = rows(CAP)
    blocks_ref[...] = jnp.broadcast_to(mine[None], blocks_ref.shape)


def settle_kernel(pieces_ref, rows_ref, target_ref, blocks_ref):
    total = pieces_ref[0].astype(F32)
    for i in range(1, pieces_ref.shape[0]):
        total += pieces_ref[i].astype(F32)
    output = rows_ref[...].astype(F32) + total.astype(BF16).astype(F32)
    residual = (output - target_ref[...].astype(F32)).astype(BF16)
    blocks_ref[...] = jnp.broadcast_to(residual[None], blocks_ref.shape)


def own_kernel(ids_ref, lengths_ref, tokens_ref, target_ref, own_ref, chosen_ref):
    row_len = tokens_ref.shape[0]
    chosen = one_hot(slot_matrix(ids_ref[...], lengths_ref[...], chosen_ref.shape[0], CAP))
    taken = times_rows(chosen, jnp.ones((chosen.shape[0], 128), BF16))[:, :1]
    live = iota((row_len, 1), 0) < jnp.sum(lengths_ref[...], axis=1, keepdims=True)
    own = tokens_ref[...].astype(F32) - target_ref[...].astype(F32)
    own_ref[...] = jnp.where(live & (taken == 0.0), own, 0.0).astype(BF16)
    chosen_ref[...] = chosen


def combine_kernel(own_ref, chosen_ref, pieces_ref, out_ref):
    slots = pieces_ref[0].astype(F32)
    for i in range(1, pieces_ref.shape[0]):
        slots += pieces_ref[i].astype(F32)
    routed = times_rows(chosen_ref[...], slots.astype(BF16))
    out_ref[...] = (own_ref[...].astype(F32) + routed).astype(BF16)


def times_rows(left, right):
    return lax.dot_general(left, right, CONTRACT_ROWS, preferred_element_type=F32)


def array(*shape, dtype=BF16):
    return jax.ShapeDtypeStruct(shape, dtype)


def swap(value):
    return lax.ppermute(value, "c", SWAP)


def pair(value):
    return lax.ppermute(value, "x", PAIR)


def cross(value):
    return lax.ppermute(value, "x", CROSS)


def after(*values):
    return lax.optimization_barrier(values)


def over_y(blocks):
    return lax.all_to_all(blocks, "y", 0, 0, tiled=True)


def over_two_columns(blocks):
    return lax.all_to_all(blocks, ("x", "y"), 0, 0, axis_index_groups=TWO_COLUMNS, tiled=True)


def in_order(mine, theirs):
    lower = lax.axis_index("x") < NX // 2
    return jnp.where(lower, mine, theirs), jnp.where(lower, theirs, mine)


def times(left, right):
    return jnp.dot(left, right, preferred_element_type=F32)


def times_t(left, right):
    return lax.dot_general(left, right, CONTRACT_COLS, preferred_element_type=F32)


def stack(*parts):
    return jnp.concatenate(parts, axis=0)


def beside(*parts):
    return jnp.concatenate(parts, axis=1)


def weight_grad(left, right):
    return times_rows(left, right).astype(BF16)


def local(tokens, target, expert_ids, doc_lengths, w_gate, w_up, w_down):
    row_len, features = tokens.shape
    slot_count = NZ * CAP
    column_rows = NY * slot_count
    gate_w, up_w, down_w = w_gate[0], w_up[0], w_down[0]
    units = gate_w.shape[1]
    ids = expert_ids.reshape(1, row_len)

    message = pl.pallas_call(dispatch_kernel, out_shape=array(NZ, 4 * CAP, features // 2))(
        ids, doc_lengths, tokens, target
    )
    arrived = lax.all_to_all(message, "z", 0, 0, tiled=True)
    blocks, my_rows, my_target = pl.pallas_call(
        arrive_kernel,
        out_shape=(array(NY, slot_count, features), array(slot_count, features), array(slot_count, features)),
    )(arrived)

    blocks, gate_w_p = after(blocks, pair(gate_w))
    column = over_y(blocks).reshape(column_rows, features)
    column, up_w_p = after(column, pair(up_w))

    def products(rows):
        return beside(*[times(rows, w).astype(BF16) for w in (gate_w, up_w, gate_w_p, up_w_p)])

    crossed = cross(column)
    part = stack(*in_order(products(column), products(crossed)))
    rows0, rows1 = in_order(column, crossed)
    part, down_w_p = after(part, pair(down_w))
    sums = part.astype(F32) + swap(part).astype(F32)
    gate, up, gate_p, up_p = jnp.split(sums, 4, axis=1)
    hidden = (jax.nn.silu(gate) * up).astype(BF16)
    hidden_p = (jax.nn.silu(gate_p) * up_p).astype(BF16)

    def output_part(s):
        return times(hidden[s], down_w) + times(hidden_p[s], down_w_p)

    partial = output_part(slice(None)).astype(BF16)
    partial, tokens_late, target_late = after(partial, tokens, target)
    own, chosen = pl.pallas_call(own_kernel, out_shape=(array(row_len, features), array(slot_count, row_len)))(
        ids, doc_lengths, tokens_late, target_late
    )
    pieces = over_two_columns(partial.reshape(2 * NY, slot_count, features))
    pieces, own, chosen = after(pieces, own, chosen)
    blocks = pl.pallas_call(settle_kernel, out_shape=array(2 * NY, slot_count, features))(pieces, my_rows, my_target)
    blocks, pair_column = after(blocks, pair(rows0))

    both = over_two_columns(blocks).reshape(2 * column_rows, features)
    both, pair_crossed = after(both, pair(rows1))
    grad_column, _ = in_order(both[:column_rows], both[column_rows:])
    part = beside(*[times_t(both, w).astype(BF16) for w in (down_w, down_w_p)])
    down_part, down_part_p = [
        times_rows(h, both) for h in (hidden, hidden_p)
    ]
    sums = part.astype(F32) + swap(part).astype(F32)
    back, back_p = jnp.split(sums, 2, axis=1)
    gate_grad = (back * up * silu_slope(gate)).astype(BF16)
    up_grad = (back * jax.nn.silu(gate)).astype(BF16)
    gate_grad_p = (back_p * up_p * silu_slope(gate_p)).astype(BF16)
    up_grad_p = (back_p * jax.nn.silu(gate_p)).astype(BF16)

    in_grads = beside(gate_grad, up_grad, gate_grad_p, up_grad_p)
    mine, theirs = in_order(in_grads[:column_rows], in_grads[column_rows:])

    def input_part(grads):
        grads = jnp.split(grads, 4, axis=1)
        own = times_t(grads[0], gate_w) + times_t(grads[1], up_w)
        return own + times_t(grads[2], gate_w_p) + times_t(grads[3], up_w_p)

    at_home = (jnp.arange(column_rows) // slot_count) == lax.axis_index("y")
    extra = jnp.where(at_home[:, None], grad_column.astype(F32), 0.0)
    partial = input_part(theirs).astype(BF16)
    partial, down_part_late = after(partial, down_part_p.astype(BF16))
    column_in = input_part(mine) + extra + cross(partial).astype(F32)
    pair_down = pair(down_part_late)
    column_in, pair_in = column_in.astype(BF16), pair(beside(gate_grad_p, up_grad_p))
    pieces = lax.all_to_all(column_in.reshape(NY * NZ, CAP, features), ("y", "z"), 0, 0, tiled=True)
    grad_tokens = pl.pallas_call(combine_kernel, out_shape=array(row_len, features))(
        own, chosen, pieces.reshape(NY, slot_count, features)
    )

    rows = stack(rows0, rows1, pair_column, pair_crossed)
    grad_down = (down_part + pair_down.astype(F32)).astype(BF16)
    grad_gate = weight_grad(rows, stack(gate_grad, pair_in[:, :units]))
    grad_up = weight_grad(rows, stack(up_grad, pair_in[:, units:]))
    return (grad_tokens, grad_gate[None], grad_up[None], grad_down[None])


def solution(mesh):
    cube = Mesh(mesh.devices.reshape(NX, NY, NZ, 2), ("x", "y", "z", "c"))
    token_spec = P(("x", "y", "z"), "c")
    in_spec, out_spec = P("z", "c", ("x", "y")), P("z", ("x", "y"), "c")
    return jax.shard_map(
        local,
        mesh=cube,
        in_specs=(token_spec, token_spec, P(("x", "y", "z")), P(("x", "y", "z"), None), in_spec, in_spec, out_spec),
        out_specs=(token_spec, in_spec, in_spec, out_spec),
        check_vma=False,
    )
```

```python
import jax
import jax.numpy as jnp
from jax import lax
from jax.experimental import pallas as pl
from jax.experimental.pallas import tpu as pltpu
from jax.sharding import Mesh, PartitionSpec as P

CAP = 2
NX, NY, NZ = 4, 8, 8
F32, BF16 = jnp.float32, jnp.bfloat16
CONTRACT_ROWS = (((0,), (0,)), ((), ()))
CONTRACT_COLS = (((1,), (1,)), ((), ()))
SWAP = [(0, 1), (1, 0)]
PAIR = [(0, 1), (1, 0), (2, 3), (3, 2)]
CROSS = [(0, 3), (3, 0), (1, 2), (2, 1)]
TWO_COLUMNS = [[x * NY + y for x in columns for y in range(NY)] for columns in ((0, 3), (1, 2))]


def silu_slope(gate_val):
    sig = jax.nn.sigmoid(gate_val)
    return sig * (1.0 + gate_val * (1.0 - sig))


def iota(shape, dim):
    return lax.broadcasted_iota(jnp.int32, shape, dim)


def one_hot(mask):
    return jnp.where(mask, 1.0, 0.0).astype(BF16)


def slot_matrix(ids, lengths, count, per_expert):
    tokens = ids.shape[1]
    slot = iota((count, tokens), 0)
    mine = ids == slot // per_expert
    before = iota((tokens, tokens), 0) < iota((tokens, tokens), 1)
    rank = jnp.dot(one_hot(mine), one_hot(before), preferred_element_type=F32)
    live = iota((count, tokens), 1) < jnp.sum(lengths, axis=1, keepdims=True)
    return mine & live & (rank == (slot % CAP).astype(F32))


def dispatch_kernel(ids_ref, lengths_ref, tokens_ref, target_ref, out_ref):
    experts, lines, half = out_ref.shape
    chosen = slot_matrix(ids_ref[...], lengths_ref[...], experts * lines, lines)
    line = iota(chosen.shape, 0) % lines
    from_target = line % (2 * CAP) >= CAP
    pick_tokens, pick_target = one_hot(chosen & ~from_target), one_hot(chosen & from_target)

    def moved(cols):
        out = jnp.dot(pick_tokens, tokens_ref[:, cols], preferred_element_type=F32)
        return out + jnp.dot(pick_target, target_ref[:, cols], preferred_element_type=F32)

    first = iota((experts * lines, half), 0) % lines < 2 * CAP
    both = jnp.where(first, moved(slice(0, half)), moved(slice(half, 2 * half)))
    out_ref[...] = both.reshape(experts, lines, half).astype(BF16)


def arrive_kernel(arrived_ref, blocks_ref, rows_ref, target_ref):
    experts, lines, half = arrived_ref.shape
    count = rows_ref.shape[0]
    arrived = arrived_ref[...].astype(F32).reshape(experts * lines, half).astype(BF16)
    row, line = iota((count, experts * lines), 0), iota((count, experts * lines), 1)

    def rows(offset):
        parts = []
        for start in (offset, offset + 2 * CAP):
            pick = one_hot(line == row // CAP * lines + row % CAP + start)
            parts.append(jnp.dot(pick, arrived, preferred_element_type=F32).astype(BF16))
        return jnp.concatenate(parts, axis=1)

    mine = rows(0)
    rows_ref[...] = mine
    target_ref[...] = rows(CAP)
    blocks_ref[...] = jnp.broadcast_to(mine[None], blocks_ref.shape)


def own_kernel(ids_ref, lengths_ref, tokens_ref, target_ref, own_ref, chosen_ref):
    row_len = tokens_ref.shape[0]
    chosen = one_hot(slot_matrix(ids_ref[...], lengths_ref[...], chosen_ref.shape[0], CAP))
    taken = times_rows(chosen, jnp.ones((chosen.shape[0], 128), BF16))[:, :1]
    live = iota((row_len, 1), 0) < jnp.sum(lengths_ref[...], axis=1, keepdims=True)
    own = tokens_ref[...].astype(F32) - target_ref[...].astype(F32)
    own_ref[...] = jnp.where(live & (taken == 0.0), own, 0.0).astype(BF16)
    chosen_ref[...] = chosen


def times_rows(left, right):
    return lax.dot_general(left, right, CONTRACT_ROWS, preferred_element_type=F32)


def array(*shape, dtype=BF16):
    return jax.ShapeDtypeStruct(shape, dtype)


def swap(value):
    return lax.ppermute(value, "c", SWAP)


def pair(value):
    return lax.ppermute(value, "x", PAIR)


def cross(value):
    return lax.ppermute(value, "x", CROSS)


def after(*values):
    return lax.optimization_barrier(values)


def over_y(blocks):
    return lax.all_to_all(blocks, "y", 0, 0, tiled=True)


def over_two_columns(blocks):
    return lax.all_to_all(blocks, ("x", "y"), 0, 0, axis_index_groups=TWO_COLUMNS, tiled=True)


def in_order(mine, theirs):
    lower = lax.axis_index("x") < NX // 2
    return jnp.where(lower, mine, theirs), jnp.where(lower, theirs, mine)


def times(left, right):
    return jnp.dot(left, right, preferred_element_type=F32)


def times_t(left, right):
    return lax.dot_general(left, right, CONTRACT_COLS, preferred_element_type=F32)


def stack(*parts):
    return jnp.concatenate(parts, axis=0)


def beside(*parts):
    return jnp.concatenate(parts, axis=1)


def weight_grad(left, right):
    return times_rows(left, right).astype(BF16)


def local(tokens, target, expert_ids, doc_lengths, w_gate, w_up, w_down):
    row_len, features = tokens.shape
    slot_count = NZ * CAP
    column_rows = NY * slot_count
    gate_w, up_w, down_w = w_gate[0], w_up[0], w_down[0]
    units = gate_w.shape[1]
    ids = expert_ids.reshape(1, row_len)

    message = pl.pallas_call(dispatch_kernel, out_shape=array(NZ, 4 * CAP, features // 2))(
        ids, doc_lengths, tokens, target
    )
    arrived = lax.all_to_all(message, "z", 0, 0, tiled=True)
    blocks, my_rows, my_target = pl.pallas_call(
        arrive_kernel,
        out_shape=(array(NY, slot_count, features), array(slot_count, features), array(slot_count, features)),
    )(arrived)

    blocks, gate_w_p = after(blocks, pair(gate_w))
    column = over_y(blocks).reshape(column_rows, features)
    column, up_w_p = after(column, pair(up_w))

    def products(rows):
        return beside(*[times(rows, w).astype(BF16) for w in (gate_w, up_w, gate_w_p, up_w_p)])

    crossed = cross(column)
    part = stack(*in_order(products(column), products(crossed)))
    rows0, rows1 = in_order(column, crossed)
    part, down_w_p = after(part, pair(down_w))
    sums = part.astype(F32) + swap(part).astype(F32)
    gate, up, gate_p, up_p = jnp.split(sums, 4, axis=1)
    hidden = (jax.nn.silu(gate) * up).astype(BF16)
    hidden_p = (jax.nn.silu(gate_p) * up_p).astype(BF16)

    def output_part(s):
        return times(hidden[s], down_w) + times(hidden_p[s], down_w_p)

    partial = output_part(slice(None)).astype(BF16)
    partial, tokens_late, target_late = after(partial, tokens, target)
    own, chosen = pl.pallas_call(own_kernel, out_shape=(array(row_len, features), array(slot_count, row_len)))(
        ids, doc_lengths, tokens_late, target_late
    )
    pieces = over_two_columns(partial.reshape(2 * NY, slot_count, features))
    pieces, own, chosen = after(pieces, own, chosen)
    expert_rows = jnp.sum(pieces.astype(F32), axis=0).astype(BF16)
    residual = (my_rows.astype(F32) + expert_rows.astype(F32) - my_target.astype(F32)).astype(BF16)
    blocks = jnp.broadcast_to(residual[None], pieces.shape)
    blocks, pair_column = after(blocks, pair(rows0))

    both = over_two_columns(blocks).reshape(2 * column_rows, features)
    both, pair_crossed = after(both, pair(rows1))
    grad_column, _ = in_order(both[:column_rows], both[column_rows:])
    part = beside(*[times_t(both, w).astype(BF16) for w in (down_w, down_w_p)])
    down_part, down_part_p = [
        times_rows(h, both) for h in (hidden, hidden_p)
    ]
    sums = part.astype(F32) + swap(part).astype(F32)
    back, back_p = jnp.split(sums, 2, axis=1)
    gate_grad = (back * up * silu_slope(gate)).astype(BF16)
    up_grad = (back * jax.nn.silu(gate)).astype(BF16)
    gate_grad_p = (back_p * up_p * silu_slope(gate_p)).astype(BF16)
    up_grad_p = (back_p * jax.nn.silu(gate_p)).astype(BF16)

    in_grads = beside(gate_grad, up_grad, gate_grad_p, up_grad_p)
    mine, theirs = in_order(in_grads[:column_rows], in_grads[column_rows:])

    def input_part(grads):
        grads = jnp.split(grads, 4, axis=1)
        own = times_t(grads[0], gate_w) + times_t(grads[1], up_w)
        return own + times_t(grads[2], gate_w_p) + times_t(grads[3], up_w_p)

    at_home = (jnp.arange(column_rows) // slot_count) == lax.axis_index("y")
    extra = jnp.where(at_home[:, None], grad_column.astype(F32), 0.0)
    partial = input_part(theirs).astype(BF16)
    half = features // 2
    partial, first, second = after(
        partial,
        beside(gate_grad_p, up_grad_p, down_part_p[:, :half].astype(BF16)),
        down_part_p[:, half:].astype(BF16),
    )
    column_in = input_part(mine) + extra + cross(partial).astype(F32)
    column_in, pair_in, pair_rest = column_in.astype(BF16), pair(first), pair(second)
    pieces = lax.all_to_all(column_in.reshape(NY * NZ, CAP, features), ("y", "z"), 0, 0, tiled=True)
    slots = jnp.sum(pieces.reshape(NY, slot_count, features).astype(F32), axis=0).astype(BF16)
    grad_tokens = (own.astype(F32) + times_rows(chosen, slots)).astype(BF16)

    rows = stack(rows0, rows1, pair_column, pair_crossed)
    pair_down = beside(pair_in[:, 2 * units :], pair_rest)
    grad_down = (down_part + pair_down.astype(F32)).astype(BF16)
    grad_gate = weight_grad(rows, stack(gate_grad, pair_in[:, :units]))
    grad_up = weight_grad(rows, stack(up_grad, pair_in[:, units : 2 * units]))
    return (grad_tokens, grad_gate[None], grad_up[None], grad_down[None])


def solution(mesh):
    cube = Mesh(mesh.devices.reshape(NX, NY, NZ, 2), ("x", "y", "z", "c"))
    token_spec = P(("x", "y", "z"), "c")
    in_spec, out_spec = P("z", "c", ("x", "y")), P("z", ("x", "y"), "c")
    return jax.shard_map(
        local,
        mesh=cube,
        in_specs=(token_spec, token_spec, P(("x", "y", "z")), P(("x", "y", "z"), None), in_spec, in_spec, out_spec),
        out_specs=(token_spec, in_spec, in_spec, out_spec),
        check_vma=False,
    )
```

```python
import jax
import jax.numpy as jnp
from jax import lax
from jax.experimental import pallas as pl
from jax.experimental.pallas import tpu as pltpu
from jax.sharding import Mesh, PartitionSpec as P

CAP = 2
NX, NY, NZ = 4, 8, 8
F32, BF16 = jnp.float32, jnp.bfloat16
CONTRACT_ROWS = (((0,), (0,)), ((), ()))
CONTRACT_COLS = (((1,), (1,)), ((), ()))
SWAP = [(0, 1), (1, 0)]
PAIR = [(0, 1), (1, 0), (2, 3), (3, 2)]
CROSS = [(0, 3), (3, 0), (1, 2), (2, 1)]
TWO_COLUMNS = [[x * NY + y for x in columns for y in range(NY)] for columns in ((0, 3), (1, 2))]


def silu_slope(gate_val):
    sig = jax.nn.sigmoid(gate_val)
    return sig * (1.0 + gate_val * (1.0 - sig))


def iota(shape, dim):
    return lax.broadcasted_iota(jnp.int32, shape, dim)


def one_hot(mask):
    return jnp.where(mask, 1.0, 0.0).astype(BF16)


def slot_matrix(ids, lengths, count, per_expert):
    tokens = ids.shape[1]
    slot = iota((count, tokens), 0)
    mine = ids == slot // per_expert
    before = iota((tokens, tokens), 0) < iota((tokens, tokens), 1)
    rank = jnp.dot(one_hot(mine), one_hot(before), preferred_element_type=F32)
    live = iota((count, tokens), 1) < jnp.sum(lengths, axis=1, keepdims=True)
    return mine & live & (rank == (slot % CAP).astype(F32))


def dispatch_kernel(ids_ref, lengths_ref, tokens_ref, target_ref, out_ref):
    experts, lines, half = out_ref.shape
    chosen = slot_matrix(ids_ref[...], lengths_ref[...], experts * lines, lines)
    line = iota(chosen.shape, 0) % lines
    from_target = line % (2 * CAP) >= CAP
    pick_tokens, pick_target = one_hot(chosen & ~from_target), one_hot(chosen & from_target)

    def moved(cols):
        out = jnp.dot(pick_tokens, tokens_ref[:, cols], preferred_element_type=F32)
        return out + jnp.dot(pick_target, target_ref[:, cols], preferred_element_type=F32)

    first = iota((experts * lines, half), 0) % lines < 2 * CAP
    both = jnp.where(first, moved(slice(0, half)), moved(slice(half, 2 * half)))
    out_ref[...] = both.reshape(experts, lines, half).astype(BF16)


def arrive_kernel(arrived_ref, blocks_ref, rows_ref, target_ref):
    experts, lines, half = arrived_ref.shape
    count = rows_ref.shape[0]
    arrived = arrived_ref[...].astype(F32).reshape(experts * lines, half).astype(BF16)
    row, line = iota((count, experts * lines), 0), iota((count, experts * lines), 1)

    def rows(offset):
        parts = []
        for start in (offset, offset + 2 * CAP):
            pick = one_hot(line == row // CAP * lines + row % CAP + start)
            parts.append(jnp.dot(pick, arrived, preferred_element_type=F32).astype(BF16))
        return jnp.concatenate(parts, axis=1)

    mine = rows(0)
    rows_ref[...] = mine
    target_ref[...] = rows(CAP)
    blocks_ref[...] = jnp.broadcast_to(mine[None], blocks_ref.shape)


def own_kernel(ids_ref, lengths_ref, tokens_ref, target_ref, own_ref, chosen_ref):
    row_len = tokens_ref.shape[0]
    chosen = one_hot(slot_matrix(ids_ref[...], lengths_ref[...], chosen_ref.shape[0], CAP))
    taken = times_rows(chosen, jnp.ones((chosen.shape[0], 128), BF16))[:, :1]
    live = iota((row_len, 1), 0) < jnp.sum(lengths_ref[...], axis=1, keepdims=True)
    own = tokens_ref[...].astype(F32) - target_ref[...].astype(F32)
    own_ref[...] = jnp.where(live & (taken == 0.0), own, 0.0).astype(BF16)
    chosen_ref[...] = chosen


def times_rows(left, right):
    return lax.dot_general(left, right, CONTRACT_ROWS, preferred_element_type=F32)


def array(*shape, dtype=BF16):
    return jax.ShapeDtypeStruct(shape, dtype)


def swap(value):
    return lax.ppermute(value, "c", SWAP)


def pair(value):
    return lax.ppermute(value, "x", PAIR)


def cross(value):
    return lax.ppermute(value, "x", CROSS)


def after(*values):
    return lax.optimization_barrier(values)


def over_y(blocks):
    return lax.all_to_all(blocks, "y", 0, 0, tiled=True)


def over_two_columns(blocks):
    return lax.all_to_all(blocks, ("x", "y"), 0, 0, axis_index_groups=TWO_COLUMNS, tiled=True)


def in_order(mine, theirs):
    lower = lax.axis_index("x") < NX // 2
    return jnp.where(lower, mine, theirs), jnp.where(lower, theirs, mine)


def times(left, right):
    return jnp.dot(left, right, preferred_element_type=F32)


def times_t(left, right):
    return lax.dot_general(left, right, CONTRACT_COLS, preferred_element_type=F32)


def stack(*parts):
    return jnp.concatenate(parts, axis=0)


def beside(*parts):
    return jnp.concatenate(parts, axis=1)


def weight_grad(left, right):
    return times_rows(left, right).astype(BF16)


def local(tokens, target, expert_ids, doc_lengths, w_gate, w_up, w_down):
    row_len, features = tokens.shape
    slot_count = NZ * CAP
    column_rows = NY * slot_count
    gate_w, up_w, down_w = w_gate[0], w_up[0], w_down[0]
    units = gate_w.shape[1]
    ids = expert_ids.reshape(1, row_len)

    message = pl.pallas_call(dispatch_kernel, out_shape=array(NZ, 4 * CAP, features // 2))(
        ids, doc_lengths, tokens, target
    )
    arrived = lax.all_to_all(message, "z", 0, 0, tiled=True)
    blocks, my_rows, my_target = pl.pallas_call(
        arrive_kernel,
        out_shape=(array(NY, slot_count, features), array(slot_count, features), array(slot_count, features)),
    )(arrived)

    blocks, gate_w_p = after(blocks, pair(gate_w))
    column = over_y(blocks).reshape(column_rows, features)
    column, up_w_p = after(column, pair(up_w))

    def products(rows):
        return beside(*[times(rows, w).astype(BF16) for w in (gate_w, up_w, gate_w_p, up_w_p)])

    crossed = cross(column)
    part = stack(*in_order(products(column), products(crossed)))
    rows0, rows1 = in_order(column, crossed)
    part, down_w_p = after(part, pair(down_w))
    sums = part.astype(F32) + swap(part).astype(F32)
    gate, up, gate_p, up_p = jnp.split(sums, 4, axis=1)
    hidden = (jax.nn.silu(gate) * up).astype(BF16)
    hidden_p = (jax.nn.silu(gate_p) * up_p).astype(BF16)

    def output_part(s):
        return times(hidden[s], down_w) + times(hidden_p[s], down_w_p)

    partial = output_part(slice(None)).astype(BF16)
    partial, tokens_late, target_late = after(partial, tokens, target)
    own, chosen = pl.pallas_call(own_kernel, out_shape=(array(row_len, features), array(slot_count, row_len)))(
        ids, doc_lengths, tokens_late, target_late
    )
    pieces = over_two_columns(partial.reshape(2 * NY, slot_count, features))
    pieces, own, chosen = after(pieces, own, chosen)
    expert_rows = jnp.sum(pieces.astype(F32), axis=0).astype(BF16)
    residual = (my_rows.astype(F32) + expert_rows.astype(F32) - my_target.astype(F32)).astype(BF16)
    blocks = jnp.broadcast_to(residual[None], pieces.shape)
    blocks, pair_column = after(blocks, pair(rows0))

    both = over_two_columns(blocks).reshape(2 * column_rows, features)
    both, pair_crossed = after(both, pair(rows1))
    grad_column, _ = in_order(both[:column_rows], both[column_rows:])
    part = beside(*[times_t(both, w).astype(BF16) for w in (down_w, down_w_p)])
    down_part, down_part_p = [
        times_rows(h, both) for h in (hidden, hidden_p)
    ]
    sums = part.astype(F32) + swap(part).astype(F32)
    back, back_p = jnp.split(sums, 2, axis=1)
    gate_grad = (back * up * silu_slope(gate)).astype(BF16)
    up_grad = (back * jax.nn.silu(gate)).astype(BF16)
    gate_grad_p = (back_p * up_p * silu_slope(gate_p)).astype(BF16)
    up_grad_p = (back_p * jax.nn.silu(gate_p)).astype(BF16)

    in_grads = beside(gate_grad, up_grad, gate_grad_p, up_grad_p)
    mine, theirs = in_order(in_grads[:column_rows], in_grads[column_rows:])

    def input_part(grads):
        grads = jnp.split(grads, 4, axis=1)
        own = times_t(grads[0], gate_w) + times_t(grads[1], up_w)
        return own + times_t(grads[2], gate_w_p) + times_t(grads[3], up_w_p)

    at_home = (jnp.arange(column_rows) // slot_count) == lax.axis_index("y")
    extra = jnp.where(at_home[:, None], grad_column.astype(F32), 0.0)
    partial = input_part(theirs).astype(BF16)
    half = features // 2
    partial, first, second = after(
        partial,
        beside(gate_grad_p, up_grad_p, down_part_p[:, :half].astype(BF16)),
        down_part_p[:, half:].astype(BF16),
    )
    column_in = input_part(mine) + extra + cross(partial).astype(F32)
    column_in, pair_in, pair_rest = column_in.astype(BF16), pair(first), pair(second)
    pieces = lax.all_to_all(column_in, ("y", "z"), 0, 0, tiled=True)
    slots = jnp.sum(pieces.reshape(NY, slot_count, features).astype(F32), axis=0).astype(BF16)
    grad_tokens = (own.astype(F32) + times_rows(chosen, slots)).astype(BF16)

    rows = stack(rows0, rows1, pair_column, pair_crossed)
    pair_down = beside(pair_in[:, 2 * units :], pair_rest)
    grad_down = (down_part + pair_down.astype(F32)).astype(BF16)
    grad_gate = weight_grad(rows, stack(gate_grad, pair_in[:, :units]))
    grad_up = weight_grad(rows, stack(up_grad, pair_in[:, units : 2 * units]))
    return (grad_tokens, grad_gate[None], grad_up[None], grad_down[None])


def solution(mesh):
    cube = Mesh(mesh.devices.reshape(NX, NY, NZ, 2), ("x", "y", "z", "c"))
    token_spec = P(("x", "y", "z"), "c")
    in_spec, out_spec = P("z", "c", ("x", "y")), P("z", ("x", "y"), "c")
    return jax.shard_map(
        local,
        mesh=cube,
        in_specs=(token_spec, token_spec, P(("x", "y", "z")), P(("x", "y", "z"), None), in_spec, in_spec, out_spec),
        out_specs=(token_spec, in_spec, in_spec, out_spec),
        check_vma=False,
    )
```
